512 devices in a mesh: env: 64 (over x, z_lo, core), row: 8 (over y, z_hi).
Axes of the slice: x: 4, y: 4, z: 16 (z_hi: 2, z_lo: 8; z = z_hi * 8 + z_lo), core: 2. Of those that a mesh axis runs over, the one named last changes fastest.
Arguments:
- descriptors: bfloat16 [131072, 1024], P(('env', 'row')), may hold values from -6 to 6
- directions: bfloat16 [64, 131072], P(None, ('env', 'row')), may hold values from -6 to 6
- ridge: float32 [64], replicated, may hold values from 0.5 to 2
- partner: int32 [2, 64], replicated, may hold values from 0 to 63, as said below
Outputs:
- image: float32 [64, 131072], P(None, ('env', 'row'))
The draws below stay inside these ranges and needn't reach their ends.
Inputs may be any that keep to these rules, and one draw needn't show every extreme that they name: For each round r there is a mask m_r, 1 to 63, the same for all blocks, with partner[r, b] = b XOR m_r; the masks of different rounds differ.
All inputs are finite; a program needn't handle non-finite values.
Results may differ from the reference program's by a relative error of at most 0.0029.
Values may be sent and summed in bfloat16 or wider, within the bound.
No kernel may reach another device: no remote copies, remote signals or barrier semaphores. Data moves between devices by JAX's collectives and lax.ppermute only.
A program may use at most 64 MiB of HBM per device.

```python
import math
import jax
import jax.numpy as jnp
from jax import lax

DESC = 1024
RHS = 64
ROUNDS = 2
BLOCKS = 64
BLOCK_ROWS = 2048
ENVS = 131072


def draw_partner(key, part):
    key = jax.random.fold_in(key, 7)
    masks = (jax.random.permutation(key, BLOCKS - 1)[:ROUNDS] + 1).astype(jnp.int32)
    indices = jnp.arange(BLOCKS, dtype=jnp.int32)
    return jnp.bitwise_xor(indices[None, :], masks[:, None]).astype(jnp.int32)


def levels(own_key, shape, split, smallest, high):
    factor_of = 1.0
    for axis_at, parts in split:
        heights = jax.random.uniform(jax.random.fold_in(jax.random.fold_in(own_key, 6), axis_at), (parts,), jnp.float32, smallest / len(split), high / len(split))
        factor_of = factor_of * jnp.repeat(jnp.exp(heights), shape[axis_at] // parts).reshape((-1,) + (1,) * (len(shape) - 1 - axis_at))
    return factor_of


def noise(key, extent, deviation, bound, pieces=(), kind=jnp.bfloat16):
    entries = jax.random.normal(key, extent, jnp.float32) * deviation
    if len(pieces) > 0:
        entries = levels(key, extent, pieces, -0.22, 0.18) * entries
    return jnp.clip(entries, min=-bound, max=bound).astype(kind)


def setup_inputs(seed: int = 0) -> dict:
    keys = jax.random.split(jax.random.key(seed), 5)
    descriptors = noise(keys[0], (ENVS, DESC), 1.0, 6.0, ((0, 512),))
    directions = noise(keys[1], (RHS, ENVS), 1.0, 6.0, ((1, 512),))
    ridge = jnp.clip(jnp.exp(jax.random.uniform(keys[2], (RHS,), jnp.float32, math.log(0.5), math.log(2.0))), 0.5, 2.0)
    partner = draw_partner(jax.random.fold_in(keys[4], 71), 0)
    return dict(descriptors=descriptors, directions=directions, ridge=ridge, partner=partner)


def kernel_block(left_rows, right_rows):
    gram_tile = jnp.dot(left_rows, right_rows.T, preferred_element_type=jnp.float32)
    shifted = 1.0 + gram_tile * (DESC ** -0.5)
    return (shifted * shifted).astype(jnp.bfloat16)


def reference(descriptors, directions, ridge, partner):
    def one_block(block_index):
        own_desc = lax.dynamic_slice(descriptors, (block_index * BLOCK_ROWS, jnp.int32(0)), (BLOCK_ROWS, DESC))
        summed = jnp.zeros((RHS, BLOCK_ROWS), jnp.float32)
        for round_index in range(ROUNDS):
            other = partner[round_index, block_index].astype(jnp.int32)
            far_desc = lax.dynamic_slice(descriptors, (other * BLOCK_ROWS, jnp.int32(0)), (BLOCK_ROWS, DESC))
            far_dirs = lax.dynamic_slice(directions, (jnp.int32(0), other * BLOCK_ROWS), (RHS, BLOCK_ROWS))
            kernel_tile = kernel_block(own_desc, far_desc)
            summed = summed + jnp.dot(far_dirs, kernel_tile.T, preferred_element_type=jnp.float32)
        return summed

    blocks = lax.map(one_block, jnp.arange(BLOCKS, dtype=jnp.int32))
    summed = jnp.transpose(blocks, (1, 0, 2)).reshape(RHS, ENVS)
    return ridge[:, None] * directions.astype(jnp.float32) + summed * ((ROUNDS * BLOCK_ROWS) ** -0.5)
```

```python
import jax
import jax.numpy as jnp
from jax import lax
from jax.sharding import PartitionSpec as P

DESC = 1024
ROUNDS = 2
AXES = ("env", "row")
ENV = 64
ROW = 8


def parity(value):
    return bin(value).count("1") & 1


def role_bits(mask):
    return 1 if mask & 1 else (mask & -mask) | 1


def out_pairs(mask):
    bits = role_bits(mask)
    pairs = []
    for env in range(ENV):
        flip = 1 - parity(env & bits)
        for row in range(ROW):
            pairs.append((env * ROW + row, (env ^ mask) * ROW + (row ^ flip)))
    return pairs


def back_pairs(mask):
    return [(target, source) for source, target in out_pairs(mask)]


def ring_pairs(shift):
    return [
        (env * ROW + row, env * ROW + (row + 2 * shift) % ROW)
        for env in range(ENV)
        for row in range(ROW)
    ]


def moved(value, pairs):
    return lax.ppermute(value, AXES, pairs)


def first_branch(mask):
    def branch(desc, dirs):
        far = (moved(desc, out_pairs(mask)), moved(dirs, out_pairs(mask)))
        near = [
            (moved(desc, ring_pairs(shift)), moved(dirs, ring_pairs(shift)))
            for shift in (1, 2, 3)
        ]
        return far, near

    return branch


def second_branch(mask):
    def branch(desc, dirs):
        return moved(desc, out_pairs(mask)), moved(dirs, out_pairs(mask))

    return branch


def back_branch(mask):
    def branch(value):
        return moved(value, back_pairs(mask))

    return branch


def kernel_block(left_rows, right_rows):
    gram_tile = lax.dot_general(
        left_rows, right_rows, (((1,), (1,)), ((), ())), preferred_element_type=jnp.float32
    )
    shifted = 1.0 + gram_tile * DESC ** (-0.5)
    return (shifted * shifted).astype(jnp.bfloat16)


def dot(left, right, left_dim, right_dim):
    return lax.dot_general(
        left, right, (((left_dim,), (right_dim,)), ((), ())), preferred_element_type=jnp.float32
    )


def on_device(descriptors, directions, ridge, partner):
    masks = partner[:, 0]
    weight = (ROUNDS * descriptors.shape[0] * ROW) ** (-0.5)
    every = range(1, ENV)
    far0, near = lax.switch(
        masks[0] - 1, [first_branch(m) for m in every], descriptors, directions
    )
    far1 = lax.switch(masks[1] - 1, [second_branch(m) for m in every], descriptors, directions)
    group = [(descriptors, directions)] + list(near)
    to_group = [0.0] * 4
    to_far = []
    for far_desc, far_dirs in (far0, far1):
        total = 0.0
        for k, (desc, dirs) in enumerate(group):
            tile = kernel_block(desc, far_desc)
            total = total + dot(dirs, tile, 1, 0)
            to_group[k] = to_group[k] + dot(far_dirs, tile, 1, 1)
        to_far.append(total)
    result = to_group[0]
    for k in (1, 2, 3):
        result = result + moved(to_group[k], ring_pairs(4 - k))
    for r in range(ROUNDS):
        result = result + lax.switch(masks[r] - 1, [back_branch(m) for m in every], to_far[r])
    return ridge[:, None] * directions.astype(jnp.float32) + weight * result


def solution(mesh):
    return jax.shard_map(
        on_device,
        mesh=mesh,
        in_specs=(P(("env", "row"), None), P(None, ("env", "row")), P(), P()),
        out_specs=P(None, ("env", "row")),
        check_vma=False,
    )
```

```python
import jax
import jax.numpy as jnp
from jax import lax
from jax.experimental import pallas as pl
from jax.experimental.pallas import tpu as pltpu
from jax.sharding import PartitionSpec as P

DESC = 1024
ROUNDS = 2
AXES = ("env", "row")
ENV = 64
ROW = 8
GROUP = 4
SIDE = 8
STEPS = 10


def parity(value):
    return bin(value).count("1") & 1


def far_step(step):
    if step < 7:
        low = step + 1
        top = low.bit_length() - 1
        for bits in range(1, 8):
            if parity(bits & low) and bits != 1 << top:
                return low << 1, bits << 1
    return 0, {7: 1, 8: 16, 9: 32}[step]


def far_pairs(step):
    mask, bits = far_step(step)
    pairs = []
    for env in range(ENV):
        target = env ^ mask
        for row in range(ROW):
            pairs.append((env * ROW + row, target * ROW + (row ^ parity(target & bits))))
    return pairs


def back_pairs(step):
    return [(target, source) for source, target in far_pairs(step)]


def side_pairs(side):
    mask = (side >> 1) << 4 | (side & 1)
    return [(e * ROW + r, (e ^ mask) * ROW + r) for e in range(ENV) for r in range(ROW)]


def near_pairs(near):
    return [(e * ROW + r, e * ROW + (r ^ (near << 1))) for e in range(ENV) for r in range(ROW)]


def moved(value, pairs):
    return lax.ppermute(value, AXES, pairs)


def beside(value, side):
    return moved(value, side_pairs(side)) if side else value


def indices(mask):
    low = (mask >> 1) & 7
    side = (mask >> 4) << 1 | (mask & 1)
    other = jnp.where((mask & 1) == 1, 7, jnp.where((mask & 16) == 16, 8, 9))
    return jnp.where(low > 0, low - 1, other), side


def both(far, side, branch_of, *operands):
    branches = [branch_of(f, s) for f in range(STEPS) for s in range(SIDE)]
    return lax.switch(far * SIDE + side, branches, *operands)


def tiles_kernel(*refs):
    sources = refs[:6]
    to_far, to_near = refs[6:8]
    held = refs[8:14]
    sems = refs[14]
    rows = to_far.shape[2]
    copies = [pltpu.make_async_copy(s, h, sems.at[i]) for i, (s, h) in enumerate(zip(sources, held))]
    for i in (4, 5, 0, 1, 2, 3):
        copies[i].start()

    def desc(i):
        return held[i][0:rows, :]

    def dirs(i):
        return jnp.concatenate(
            [held[i][rows : rows + 16, j * rows : (j + 1) * rows] for j in range(4)], axis=0
        )

    def dot(left, right, left_dim, right_dim):
        return lax.dot_general(
            left,
            right,
            (((left_dim,), (right_dim,)), ((), ())),
            preferred_element_type=jnp.float32,
        )

    copies[4].wait()
    copies[5].wait()
    for k in range(GROUP):
        copies[k].wait()
        for r in range(ROUNDS):
            gram = dot(desc(k), desc(4 + r), 1, 1)
            shifted = 1.0 + gram * DESC ** (-0.5)
            tile = (shifted * shifted).astype(jnp.bfloat16)
            out = dot(dirs(k), tile, 1, 0)
            near = dot(dirs(4 + r), tile, 1, 1)
            if k == 0:
                to_far[r] = out
            else:
                to_far[r] += out
            if r == 0:
                to_near[k] = near
            else:
                to_near[k] += near


def tiles(group, far, rhs, rows):
    packed = jax.typeof(group[0]).shape
    return pl.pallas_call(
        tiles_kernel,
        out_shape=(
            jax.ShapeDtypeStruct((ROUNDS, rhs, rows), jnp.float32),
            jax.ShapeDtypeStruct((GROUP, rhs, rows), jnp.float32),
        ),
        in_specs=[pl.BlockSpec(memory_space=pl.ANY)] * 6,
        out_specs=(pl.BlockSpec(memory_space=pltpu.VMEM),) * 2,
        scratch_shapes=[pltpu.VMEM(packed, jnp.bfloat16)] * 6 + [pltpu.SemaphoreType.DMA((6,))],
        compiler_params=pltpu.CompilerParams(vmem_limit_bytes=32 * 1024 * 1024),
        cost_estimate=pl.CostEstimate(
            flops=8 * 2 * rows * rows * (DESC + 2 * rhs),
            bytes_accessed=6 * rows * DESC * 2,
            transcendentals=0,
        ),
    )(*group, *far)


def on_device(descriptors, directions, ridge, partner):
    rhs, rows = directions.shape
    weight = (ROUNDS * rows * ROW) ** (-0.5)
    far0, side0 = indices(partner[0, 0])
    far1, side1 = indices(partner[1, 0])
    flat = jnp.concatenate([directions[16 * j : 16 * j + 16] for j in range(4)], axis=1)
    packed = jnp.concatenate([descriptors, flat], axis=0)

    def out_first(far, side):
        def branch(value):
            first = moved(value, far_pairs(far))
            second = beside(value, side)
            return first, second, *[moved(value, near_pairs(k)) for k in (1, 2, 3)]

        return branch

    def out_second(far, side):
        def branch(first, second):
            return beside(first, side), moved(second, far_pairs(far))

        return branch

    def back_first(far, side):
        def branch(first, second):
            return beside(first, side), moved(second, back_pairs(far))

        return branch

    def back_second(far, side):
        def branch(first, second):
            return moved(first, back_pairs(far)), beside(second, side)

        return branch

    first, second, *near = both(far0, side1, out_first, packed)
    first, second = both(far1, side0, out_second, first, second)
    to_far, to_near = tiles([packed, *near], [first, second], rhs, rows)
    half = moved(to_near[2:], near_pairs(2))
    first, second = both(far1, side0, back_first, to_far[0], to_far[1])
    near_sum = to_near[:2] + half
    other = moved(near_sum[1], near_pairs(1))
    first, second = both(far0, side1, back_second, first, second)
    result = near_sum[0] + other + first + second
    return ridge[:, None] * directions.astype(jnp.float32) + weight * result


def solution(mesh):
    return jax.shard_map(
        on_device,
        mesh=mesh,
        in_specs=(P(("env", "row"), None), P(None, ("env", "row")), P(), P()),
        out_specs=P(None, ("env", "row")),
        check_vma=False,
    )
```

```python
import jax
import jax.numpy as jnp
from jax import lax
from jax.experimental import pallas as pl
from jax.experimental.pallas import tpu as pltpu
from jax.sharding import PartitionSpec as P

DESC = 1024
ROUNDS = 2
AXES = ("env", "row")
ENV = 64
ROW = 8
GROUP = 4
SIDE = 8
STEPS = 10


def parity(value):
    return bin(value).count("1") & 1


def far_step(step):
    if step < 7:
        low = step + 1
        top = low.bit_length() - 1
        for bits in range(1, 8):
            if parity(bits & low) and bits != 1 << top:
                return low << 1, bits << 1
    return 0, {7: 1, 8: 16, 9: 32}[step]


def far_pairs(step):
    mask, bits = far_step(step)
    pairs = []
    for env in range(ENV):
        target = env ^ mask
        for row in range(ROW):
            pairs.append((env * ROW + row, target * ROW + (row ^ parity(target & bits))))
    return pairs


def back_pairs(step):
    return [(target, source) for source, target in far_pairs(step)]


def side_pairs(side):
    mask = (side >> 1) << 4 | (side & 1)
    return [(e * ROW + r, (e ^ mask) * ROW + r) for e in range(ENV) for r in range(ROW)]


def near_pairs(near):
    return [(e * ROW + r, e * ROW + (r ^ (near << 1))) for e in range(ENV) for r in range(ROW)]


def moved(value, pairs):
    return lax.ppermute(value, AXES, pairs)


def beside(value, side):
    return moved(value, side_pairs(side)) if side else value


def start_kernel(partner, desc, dirs, packed, far0, side0, far1, side1, sem):
    rows = desc.shape[0]
    copy = pltpu.make_async_copy(desc, packed.at[0:rows], sem)
    copy.start()
    for r, (far, side) in enumerate(((far0, side0), (far1, side1))):
        mask = partner[r, 0]
        low = (mask >> 1) & 7
        other = jnp.where((mask & 1) == 1, 7, jnp.where((mask & 16) == 16, 8, 9))
        far[0, 0] = jnp.where(low > 0, low - 1, other)
        side[0, 0] = ((mask >> 4) << 1) | (mask & 1)
    for j in range(4):
        packed[rows : rows + 16, j * rows : (j + 1) * rows] = dirs[16 * j : 16 * j + 16, :]
    copy.wait()


def start(partner, desc, dirs):
    index = jax.ShapeDtypeStruct((1, 1), jnp.int32)
    smem = pl.BlockSpec(memory_space=pltpu.SMEM)
    vmem = pl.BlockSpec(memory_space=pltpu.VMEM)
    packed, *steps = pl.pallas_call(
        start_kernel,
        out_shape=(jax.ShapeDtypeStruct((desc.shape[0] + 16, DESC), desc.dtype),) + (index,) * 4,
        in_specs=[smem, pl.BlockSpec(memory_space=pl.ANY), vmem],
        out_specs=(vmem,) + (smem,) * 4,
        scratch_shapes=[pltpu.SemaphoreType.DMA],
    )(partner, desc, dirs)
    return packed, [step.reshape(()) for step in steps]


def together(far, side, pairs_of, far_value, side_value, *nears):
    def side_branch(step):
        return lambda value: beside(value, step)

    def far_branch(step):
        def branch(side, far_value, side_value, *values):
            near_values = [moved(v, near_pairs(k)) for v, (_, k) in zip(values, nears)]
            side_value = lax.switch(side, [side_branch(s) for s in range(SIDE)], side_value)
            return moved(far_value, pairs_of(step)), side_value, *near_values

        return branch

    branches = [far_branch(f) for f in range(STEPS)]
    return lax.switch(far, branches, side, far_value, side_value, *[v for v, _ in nears])


def tiles_kernel(*refs):
    sources = refs[:6]
    to_far, to_near = refs[6:8]
    held = refs[8:14]
    sems = refs[14]
    rows = to_far.shape[2]
    copies = [pltpu.make_async_copy(s, h, sems.at[i]) for i, (s, h) in enumerate(zip(sources, held))]
    for i in (4, 5, 0, 1, 2, 3):
        copies[i].start()

    def desc(i):
        return held[i][0:rows, :]

    def dirs(i):
        return jnp.concatenate(
            [held[i][rows : rows + 16, j * rows : (j + 1) * rows] for j in range(4)], axis=0
        )

    def dot(left, right, left_dim, right_dim):
        return lax.dot_general(
            left,
            right,
            (((left_dim,), (right_dim,)), ((), ())),
            preferred_element_type=jnp.float32,
        )

    copies[4].wait()
    copies[5].wait()
    for k in range(GROUP):
        copies[k].wait()
        for r in range(ROUNDS):
            gram = dot(desc(k), desc(4 + r), 1, 1)
            shifted = 1.0 + gram * DESC ** (-0.5)
            tile = (shifted * shifted).astype(jnp.bfloat16)
            out = dot(dirs(k), tile, 1, 0)
            near = dot(dirs(4 + r), tile, 1, 1)
            if k == 0:
                to_far[r] = out
            else:
                to_far[r] += out
            if r == 0:
                to_near[k] = near
            else:
                to_near[k] += near


def tiles(group, far, rhs, rows):
    packed = jax.typeof(group[0]).shape
    return pl.pallas_call(
        tiles_kernel,
        out_shape=(
            jax.ShapeDtypeStruct((ROUNDS, rhs, rows), jnp.float32),
            jax.ShapeDtypeStruct((GROUP, rhs, rows), jnp.float32),
        ),
        in_specs=[pl.BlockSpec(memory_space=pl.ANY)] * 6,
        out_specs=(pl.BlockSpec(memory_space=pltpu.VMEM),) * 2,
        scratch_shapes=[pltpu.VMEM(packed, jnp.bfloat16)] * 6 + [pltpu.SemaphoreType.DMA((6,))],
        compiler_params=pltpu.CompilerParams(vmem_limit_bytes=32 * 1024 * 1024),
        cost_estimate=pl.CostEstimate(
            flops=8 * 2 * rows * rows * (DESC + 2 * rhs),
            bytes_accessed=6 * rows * DESC * 2,
            transcendentals=0,
        ),
    )(*group, *far)


def on_device(descriptors, directions, ridge, partner):
    rhs, rows = directions.shape
    weight = (ROUNDS * rows * ROW) ** (-0.5)
    packed, (far0, side0, far1, side1) = start(partner, descriptors, directions)
    first, second, *near = together(
        far0, side1, far_pairs, packed, packed, (packed, 1), (packed, 2), (packed, 3)
    )
    second, first = together(far1, side0, far_pairs, second, first)
    to_far, to_near = tiles([packed, *near], [first, second], rhs, rows)
    second, first, half = together(
        far1, side0, back_pairs, to_far[1], to_far[0], (to_near[2:], 2)
    )
    to_near = to_near[:2] + half
    first, second, other = together(far0, side1, back_pairs, first, second, (to_near[1], 1))
    result = to_near[0] + other + first + second
    return ridge[:, None] * directions.astype(jnp.float32) + weight * result


def solution(mesh):
    return jax.shard_map(
        on_device,
        mesh=mesh,
        in_specs=(P(("env", "row"), None), P(None, ("env", "row")), P(), P()),
        out_specs=P(None, ("env", "row")),
        check_vma=False,
    )
```

```python
import jax
import jax.numpy as jnp
from jax import lax
from jax.experimental import pallas as pl
from jax.experimental.pallas import tpu as pltpu
from jax.sharding import PartitionSpec as P

DESC = 1024
ROUNDS = 2
AXES = ("env", "row")
ENV = 64
ROW = 8
GROUP = 4
SIDE = 8
STEPS = 10


def parity(value):
    return bin(value).count("1") & 1


def far_step(step):
    if step < 7:
        low = step + 1
        top = low.bit_length() - 1
        for bits in range(1, 8):
            if parity(bits & low) and bits != 1 << top:
                return low << 1, bits << 1
    return 0, {0: 1, 1: 16, 2: 32}[(step - 7) % 3]


def far_pairs(step):
    mask, bits = far_step(step)
    pairs = []
    for env in range(ENV):
        target = env ^ mask
        for row in range(ROW):
            pairs.append((env * ROW + row, target * ROW + (row ^ parity(target & bits))))
    return pairs


def back_pairs(step):
    if step < STEPS:
        return [(target, source) for source, target in far_pairs(step)]
    mask, bits = far_step(step)
    return [
        (env * ROW + row, env * ROW + (row ^ 1 ^ parity(env & bits)))
        for env in range(ENV)
        for row in range(ROW)
    ]


def side_pairs(side):
    mask = (side >> 1) << 4 | (side & 1)
    return [(e * ROW + r, (e ^ mask) * ROW + r) for e in range(ENV) for r in range(ROW)]


def near_groups():
    return [[2 * y + half for y in range(GROUP)] for half in range(2)]


def side_groups():
    return [[(p >> 1) << 4 | z << 1 | (p & 1) for p in range(SIDE)] for z in range(8)]


def moved(value, pairs):
    return lax.ppermute(value, AXES, pairs)


def beside(value, side):
    return moved(value, side_pairs(side)) if side else value


def start_kernel(partner, desc, dirs, packed, copies, far0, side0, far1, side1, back0, sem):
    rows = desc.shape[0]
    copy = pltpu.make_async_copy(desc, packed.at[0:rows], sem.at[0])
    copy.start()
    for r, (far, side) in enumerate(((far0, side0), (far1, side1))):
        mask = partner[r, 0]
        low = (mask >> 1) & 7
        other = jnp.where((mask & 1) == 1, 7, jnp.where((mask & 16) == 16, 8, 9))
        far[0, 0] = jnp.where(low > 0, low - 1, other)
        side[0, 0] = ((mask >> 4) << 1) | (mask & 1)
    back0[0, 0] = far0[0, 0] + jnp.where(far0[0, 0] < 7, 0, 3)
    for j in range(4):
        packed[rows : rows + 16, j * rows : (j + 1) * rows] = dirs[16 * j : 16 * j + 16, :]
    copy.wait()
    spread = [pltpu.make_async_copy(packed, copies.at[k], sem.at[1 + k]) for k in range(GROUP)]
    for copy in spread:
        copy.start()
    for copy in spread:
        copy.wait()


def start(partner, desc, dirs):
    index = jax.ShapeDtypeStruct((1, 1), jnp.int32)
    smem = pl.BlockSpec(memory_space=pltpu.SMEM)
    vmem = pl.BlockSpec(memory_space=pltpu.VMEM)
    packed, copies, *steps = pl.pallas_call(
        start_kernel,
        out_shape=(
            jax.ShapeDtypeStruct((desc.shape[0] + 16, DESC), desc.dtype),
            jax.ShapeDtypeStruct((GROUP, desc.shape[0] + 16, DESC), desc.dtype),
        )
        + (index,) * 5,
        in_specs=[smem, pl.BlockSpec(memory_space=pl.ANY), vmem],
        out_specs=(vmem, pl.BlockSpec(memory_space=pl.ANY)) + (smem,) * 5,
        scratch_shapes=[pltpu.SemaphoreType.DMA((1 + GROUP,))],
    )(partner, desc, dirs)
    return packed, copies, [step.reshape(()) for step in steps]


def dot(left, right, left_dim, right_dim):
    return lax.dot_general(
        left, right, (((left_dim,), (right_dim,)), ((), ())), preferred_element_type=jnp.float32
    )


def unpacked(flat, rows):
    return jnp.concatenate([flat[:, j * rows : (j + 1) * rows] for j in range(4)], axis=0)


def tiles_kernel(first, second, group, to_far, to_near, far, flat, held, sems):
    rhs, rows = to_far.shape[1:]
    copies = [
        pltpu.make_async_copy(first.at[0:rows], far.at[0:rows], sems.at[0]),
        pltpu.make_async_copy(second.at[0:rows], far.at[rows : 2 * rows], sems.at[1]),
        pltpu.make_async_copy(first.at[rows : rows + 16], flat.at[0], sems.at[2]),
        pltpu.make_async_copy(second.at[rows : rows + 16], flat.at[1], sems.at[3]),
    ]
    copies += [pltpu.make_async_copy(group.at[k], held.at[k], sems.at[4 + k]) for k in range(GROUP)]
    for copy in copies:
        copy.start()
    for copy in copies[:4]:
        copy.wait()
    far_dirs = jnp.concatenate([unpacked(flat[r], rows) for r in range(ROUNDS)], axis=1)
    total = jnp.zeros((rhs, 2 * rows), jnp.float32)
    for k in range(GROUP):
        copies[4 + k].wait()
        gram = dot(held[k, 0:rows, :], far[...], 1, 1)
        shifted = 1.0 + gram * DESC ** (-0.5)
        tile = (shifted * shifted).astype(jnp.bfloat16)
        total = total + dot(unpacked(held[k, rows : rows + 16, :], rows), tile, 1, 0)
        to_near[k] = dot(far_dirs, tile, 1, 1)
    to_far[0] = total[:, 0:rows].astype(to_far.dtype)
    to_far[1] = total[:, rows:].astype(to_far.dtype)


def tiles(group, first, second, rhs):
    rows = first.shape[0] - 16
    vmem = pl.BlockSpec(memory_space=pltpu.VMEM)
    hbm = pl.BlockSpec(memory_space=pl.ANY)
    return pl.pallas_call(
        tiles_kernel,
        out_shape=(
            jax.ShapeDtypeStruct((ROUNDS, rhs, rows), jnp.bfloat16),
            jax.ShapeDtypeStruct((GROUP, rhs, rows), jnp.float32),
        ),
        in_specs=[hbm] * 3,
        out_specs=(vmem, vmem),
        scratch_shapes=[
            pltpu.VMEM((2 * rows, DESC), jnp.bfloat16),
            pltpu.VMEM((ROUNDS, 16, DESC), jnp.bfloat16),
            pltpu.VMEM(group.shape, jnp.bfloat16),
            pltpu.SemaphoreType.DMA((4 + GROUP,)),
        ],
        compiler_params=pltpu.CompilerParams(vmem_limit_bytes=24 * 1024 * 1024),
        cost_estimate=pl.CostEstimate(
            flops=16 * rows * rows * (DESC + 2 * rhs),
            bytes_accessed=6 * rows * DESC * 2,
            transcendentals=0,
        ),
    )(first, second, group)


def pick(index, count, branch_of, *operands):
    return lax.switch(index, [branch_of(i) for i in range(count)], *operands)


def side_step(side, value):
    return pick(side, SIDE, lambda s: lambda v: beside(v, s), value)


def exchanged(value, axis, groups):
    return lax.all_to_all(value, axis, 0, 0, axis_index_groups=groups)


def on_device(descriptors, directions, ridge, partner):
    rhs, rows = directions.shape
    weight = (ROUNDS * rows * ROW) ** (-0.5)
    packed, copies, (far0, side0, far1, side1, back0) = start(partner, descriptors, directions)

    def out_first(far):
        def branch(value, side):
            return side_step(side, value), moved(value, far_pairs(far))

        return branch

    def out_second(far):
        def branch(first, second, copies, side):
            group = exchanged(copies, "row", near_groups())
            return group, side_step(side, first), moved(second, far_pairs(far))

        return branch

    def back_both(far):
        def branch(first, second, other_far):
            first = pick(
                other_far, STEPS + 3, lambda f: lambda v: moved(v, back_pairs(f)), first
            )
            return first, moved(second, back_pairs(far))

        return branch

    second, first = pick(far0, STEPS, out_first, packed, side1)
    group, first, second = pick(far1, STEPS, out_second, first, second, copies, side0)
    to_far, to_near = tiles(group, first, second, rhs)
    near = exchanged(to_near, "row", near_groups())
    first, second = pick(far1, STEPS, back_both, to_far[0], to_far[1], back0)
    env = lax.axis_index("env")
    place = (env >> 4) << 1 | (env & 1)
    slots = jnp.arange(SIDE, dtype=jnp.int32)[:, None, None]
    none = jnp.zeros_like(first)
    sent = jnp.where(slots == place ^ side0, first, none)
    sent = sent + jnp.where(slots == place ^ side1, second, none)
    side = exchanged(sent, "env", side_groups())
    result = jnp.sum(near, axis=0) + jnp.sum(side.astype(jnp.float32), axis=0)
    return ridge[:, None] * directions.astype(jnp.float32) + weight * result


def solution(mesh):
    return jax.shard_map(
        on_device,
        mesh=mesh,
        in_specs=(P(("env", "row"), None), P(None, ("env", "row")), P(), P()),
        out_specs=P(None, ("env", "row")),
        check_vma=False,
    )
```

```python
import jax
import jax.numpy as jnp
from jax import lax
from jax.experimental import pallas as pl
from jax.experimental.pallas import tpu as pltpu
from jax.sharding import PartitionSpec as P

DESC = 1024
ROUNDS = 2
AXES = ("env", "row")
ENV = 64
ROW = 8
GROUP = 4
SIDE = 8
STEPS = 10


def parity(value):
    return bin(value).count("1") & 1


def far_step(step):
    if step < 7:
        low = step + 1
        top = low.bit_length() - 1
        for bits in range(1, 8):
            if parity(bits & low) and bits != 1 << top:
                return low << 1, bits << 1
    return 0, {0: 1, 1: 16, 2: 32}[(step - 7) % 3]


def far_pairs(step):
    mask, bits = far_step(step)
    pairs = []
    for env in range(ENV):
        target = env ^ mask
        for row in range(ROW):
            pairs.append((env * ROW + row, target * ROW + (row ^ parity(target & bits))))
    return pairs


def back_pairs(step):
    if step < STEPS:
        return [(target, source) for source, target in far_pairs(step)]
    mask, bits = far_step(step)
    return [
        (env * ROW + row, env * ROW + (row ^ 1 ^ parity(env & bits)))
        for env in range(ENV)
        for row in range(ROW)
    ]


def side_pairs(side):
    mask = (side >> 1) << 4 | (side & 1)
    return [(e * ROW + r, (e ^ mask) * ROW + r) for e in range(ENV) for r in range(ROW)]


def near_groups():
    return [[2 * y + half for y in range(GROUP)] for half in range(2)]


def side_groups():
    return [[(p >> 1) << 4 | z << 1 | (p & 1) for p in range(SIDE)] for z in range(8)]


def moved(value, pairs):
    return lax.ppermute(value, AXES, pairs)


def beside(value, side):
    return moved(value, side_pairs(side)) if side else value


def start_kernel(partner, desc, dirs, packed, copies, far0, side0, far1, side1, sem):
    rows = desc.shape[0]
    copy = pltpu.make_async_copy(desc, packed.at[0:rows], sem.at[0])
    copy.start()
    for r, (far, side) in enumerate(((far0, side0), (far1, side1))):
        mask = partner[r, 0]
        low = (mask >> 1) & 7
        other = jnp.where((mask & 1) == 1, 7, jnp.where((mask & 16) == 16, 8, 9))
        far[0, 0] = jnp.where(low > 0, low - 1, other)
        side[0, 0] = ((mask >> 4) << 1) | (mask & 1)
    for j in range(4):
        packed[rows : rows + 16, j * rows : (j + 1) * rows] = dirs[16 * j : 16 * j + 16, :]
    copy.wait()
    spread = [pltpu.make_async_copy(packed, copies.at[k], sem.at[1 + k]) for k in range(GROUP)]
    for copy in spread:
        copy.start()
    for copy in spread:
        copy.wait()


def start(partner, desc, dirs):
    index = jax.ShapeDtypeStruct((1, 1), jnp.int32)
    smem = pl.BlockSpec(memory_space=pltpu.SMEM)
    vmem = pl.BlockSpec(memory_space=pltpu.VMEM)
    packed, copies, *steps = pl.pallas_call(
        start_kernel,
        out_shape=(
            jax.ShapeDtypeStruct((desc.shape[0] + 16, DESC), desc.dtype),
            jax.ShapeDtypeStruct((GROUP, desc.shape[0] + 16, DESC), desc.dtype),
        )
        + (index,) * 4,
        in_specs=[smem, pl.BlockSpec(memory_space=pl.ANY), vmem],
        out_specs=(vmem, pl.BlockSpec(memory_space=pl.ANY)) + (smem,) * 4,
        scratch_shapes=[pltpu.SemaphoreType.DMA((1 + GROUP,))],
    )(partner, desc, dirs)
    return packed, copies, [step.reshape(()) for step in steps]


def dot(left, right, left_dim, right_dim):
    return lax.dot_general(
        left, right, (((left_dim,), (right_dim,)), ((), ())), preferred_element_type=jnp.float32
    )


def unpacked(flat, rows):
    return jnp.concatenate([flat[:, j * rows : (j + 1) * rows] for j in range(4)], axis=0)


def tiles_kernel(first, second, group, to_far, to_near, far, flat, held, sems):
    rhs, rows = to_far.shape[1:]
    copies = [
        pltpu.make_async_copy(first.at[0:rows], far.at[0:rows], sems.at[0]),
        pltpu.make_async_copy(second.at[0:rows], far.at[rows : 2 * rows], sems.at[1]),
        pltpu.make_async_copy(first.at[rows : rows + 16], flat.at[0], sems.at[2]),
        pltpu.make_async_copy(second.at[rows : rows + 16], flat.at[1], sems.at[3]),
    ]
    copies += [pltpu.make_async_copy(group.at[k], held.at[k], sems.at[4 + k]) for k in range(GROUP)]
    for copy in copies:
        copy.start()
    for copy in copies[:4]:
        copy.wait()
    far_dirs = jnp.concatenate([unpacked(flat[r], rows) for r in range(ROUNDS)], axis=1)
    total = jnp.zeros((rhs, 2 * rows), jnp.float32)
    for k in range(GROUP):
        copies[4 + k].wait()
        gram = dot(held[k, 0:rows, :], far[...], 1, 1)
        shifted = 1.0 + gram * DESC ** (-0.5)
        tile = (shifted * shifted).astype(jnp.bfloat16)
        total = total + dot(unpacked(held[k, rows : rows + 16, :], rows), tile, 1, 0)
        to_near[k] = dot(far_dirs, tile, 1, 1)
    to_far[0] = total[:, 0:rows].astype(to_far.dtype)
    to_far[1] = total[:, rows:].astype(to_far.dtype)


def tiles(group, first, second, rhs):
    rows = first.shape[0] - 16
    vmem = pl.BlockSpec(memory_space=pltpu.VMEM)
    hbm = pl.BlockSpec(memory_space=pl.ANY)
    return pl.pallas_call(
        tiles_kernel,
        out_shape=(
            jax.ShapeDtypeStruct((ROUNDS, rhs, rows), jnp.bfloat16),
            jax.ShapeDtypeStruct((GROUP, rhs, rows), jnp.float32),
        ),
        in_specs=[hbm] * 3,
        out_specs=(vmem, vmem),
        scratch_shapes=[
            pltpu.VMEM((2 * rows, DESC), jnp.bfloat16),
            pltpu.VMEM((ROUNDS, 16, DESC), jnp.bfloat16),
            pltpu.VMEM(group.shape, jnp.bfloat16),
            pltpu.SemaphoreType.DMA((4 + GROUP,)),
        ],
        compiler_params=pltpu.CompilerParams(vmem_limit_bytes=24 * 1024 * 1024),
        cost_estimate=pl.CostEstimate(
            flops=16 * rows * rows * (DESC + 2 * rhs),
            bytes_accessed=6 * rows * DESC * 2,
            transcendentals=0,
        ),
    )(first, second, group)


def pick(index, count, branch_of, *operands):
    return lax.switch(index, [branch_of(i) for i in range(count)], *operands)


def side_step(side, value):
    return pick(side, SIDE, lambda s: lambda v: beside(v, s), value)


def exchanged(value, axis, groups):
    return lax.all_to_all(value, axis, 0, 0, axis_index_groups=groups)


def on_device(descriptors, directions, ridge, partner):
    rhs, rows = directions.shape
    weight = (ROUNDS * rows * ROW) ** (-0.5)
    packed, copies, (far0, side0, far1, side1) = start(partner, descriptors, directions)

    def out_first(far):
        def branch(value, side):
            return side_step(side, value), moved(value, far_pairs(far))

        return branch

    def out_second(far):
        def branch(first, second, copies, side):
            group = exchanged(copies, "row", near_groups())
            return group, side_step(side, first), moved(second, far_pairs(far))

        return branch

    def back_both(step):
        def branch(first, second, other):
            second = pick(other, STEPS, lambda f: lambda v: moved(v, back_pairs(f)), second)
            return second, moved(first, back_pairs(step if step < 7 else step + 3))

        return branch

    second, first = pick(far0, STEPS, out_first, packed, side1)
    group, first, second = pick(far1, STEPS, out_second, first, second, copies, side0)
    to_far, to_near = tiles(group, first, second, rhs)
    near = exchanged(to_near, "row", near_groups())
    second, first = pick(far0, STEPS, back_both, to_far[0], to_far[1], far1)
    env = lax.axis_index("env")
    place = (env >> 4) << 1 | (env & 1)
    slots = jnp.arange(SIDE, dtype=jnp.int32)[:, None, None]
    none = jnp.zeros_like(first)
    sent = jnp.where(slots == place ^ side0, first, none)
    sent = sent + jnp.where(slots == place ^ side1, second, none)
    side = exchanged(sent, "env", side_groups())
    result = jnp.sum(near, axis=0) + jnp.sum(side.astype(jnp.float32), axis=0)
    return ridge[:, None] * directions.astype(jnp.float32) + weight * result


def solution(mesh):
    return jax.shard_map(
        on_device,
        mesh=mesh,
        in_specs=(P(("env", "row"), None), P(None, ("env", "row")), P(), P()),
        out_specs=P(None, ("env", "row")),
        check_vma=False,
    )
```

```python
import jax
import jax.numpy as jnp
from jax import lax
from jax.experimental import pallas as pl
from jax.experimental.pallas import tpu as pltpu
from jax.sharding import PartitionSpec as P

DESC = 1024
ROUNDS = 2
AXES = ("env", "row")
ENV = 64
ROW = 8
GROUP = 4
SIDE = 8
STEPS = 10


def parity(value):
    return bin(value).count("1") & 1


def far_step(step):
    if step < 7:
        low = step + 1
        top = low.bit_length() - 1
        for bits in range(1, 8):
            if parity(bits & low) and bits != 1 << top:
                return low << 1, bits << 1
    return 0, {0: 1, 1: 16, 2: 32}[(step - 7) % 3]


def far_pairs(step):
    mask, bits = far_step(step)
    pairs = []
    for env in range(ENV):
        target = env ^ mask
        for row in range(ROW):
            pairs.append((env * ROW + row, target * ROW + (row ^ parity(target & bits))))
    return pairs


def back_pairs(step):
    if step < STEPS:
        return [(target, source) for source, target in far_pairs(step)]
    mask, bits = far_step(step)
    return [
        (env * ROW + row, env * ROW + (row ^ 1 ^ parity(env & bits)))
        for env in range(ENV)
        for row in range(ROW)
    ]


def side_pairs(side):
    mask = (side >> 1) << 4 | (side & 1)
    return [(e * ROW + r, (e ^ mask) * ROW + r) for e in range(ENV) for r in range(ROW)]


def second_pairs(step):
    return back_pairs(step) if step < 7 else far_pairs(step)


def second_back_pairs(step):
    return [(target, source) for source, target in second_pairs(step)]


def near_pairs(near):
    return [(e * ROW + r, e * ROW + (r ^ (near << 1))) for e in range(ENV) for r in range(ROW)]


def side_groups():
    return [[(p >> 1) << 4 | z << 1 | (p & 1) for p in range(SIDE)] for z in range(8)]


def moved(value, pairs):
    return lax.ppermute(value, AXES, pairs)


def beside(value, side):
    return moved(value, side_pairs(side)) if side else value


def start_kernel(partner, desc, dirs, packed, far0, side0, far1, side1, sem):
    rows = desc.shape[0]
    copy = pltpu.make_async_copy(desc, packed.at[0:rows], sem)
    copy.start()
    for r, (far, side) in enumerate(((far0, side0), (far1, side1))):
        mask = partner[r, 0]
        low = (mask >> 1) & 7
        other = jnp.where((mask & 1) == 1, 7, jnp.where((mask & 16) == 16, 8, 9))
        far[0, 0] = jnp.where(low > 0, low - 1, other)
        side[0, 0] = ((mask >> 4) << 1) | (mask & 1)
    for j in range(4):
        packed[rows : rows + 16, j * rows : (j + 1) * rows] = dirs[16 * j : 16 * j + 16, :]
    copy.wait()


def start(partner, desc, dirs):
    index = jax.ShapeDtypeStruct((1, 1), jnp.int32)
    smem = pl.BlockSpec(memory_space=pltpu.SMEM)
    vmem = pl.BlockSpec(memory_space=pltpu.VMEM)
    packed, *steps = pl.pallas_call(
        start_kernel,
        out_shape=(jax.ShapeDtypeStruct((desc.shape[0] + 16, DESC), desc.dtype),) + (index,) * 4,
        in_specs=[smem, pl.BlockSpec(memory_space=pl.ANY), vmem],
        out_specs=(vmem,) + (smem,) * 4,
        scratch_shapes=[pltpu.SemaphoreType.DMA],
    )(partner, desc, dirs)
    return packed, [step.reshape(()) for step in steps]


def dot(left, right, left_dim, right_dim):
    return lax.dot_general(
        left, right, (((left_dim,), (right_dim,)), ((), ())), preferred_element_type=jnp.float32
    )


def unpacked(flat, rows):
    return jnp.concatenate([flat[:, j * rows : (j + 1) * rows] for j in range(4)], axis=0)


def tiles_kernel(first, second, *refs):
    group, (to_far, to_near, far, flat, held, sems) = refs[:GROUP], refs[GROUP:]
    rhs, rows = to_far.shape[1:]
    copies = [
        pltpu.make_async_copy(first.at[0:rows], far.at[0:rows], sems.at[0]),
        pltpu.make_async_copy(second.at[0:rows], far.at[rows : 2 * rows], sems.at[1]),
        pltpu.make_async_copy(first.at[rows : rows + 16], flat.at[0], sems.at[2]),
        pltpu.make_async_copy(second.at[rows : rows + 16], flat.at[1], sems.at[3]),
    ]
    copies += [pltpu.make_async_copy(group[k], held.at[k], sems.at[4 + k]) for k in range(GROUP)]
    for copy in copies:
        copy.start()
    for copy in copies[:4]:
        copy.wait()
    far_dirs = jnp.concatenate([unpacked(flat[r], rows) for r in range(ROUNDS)], axis=1)
    total = jnp.zeros((rhs, 2 * rows), jnp.float32)
    for k in range(GROUP):
        copies[4 + k].wait()
        gram = dot(held[k, 0:rows, :], far[...], 1, 1)
        shifted = 1.0 + gram * DESC ** (-0.5)
        tile = (shifted * shifted).astype(jnp.bfloat16)
        total = total + dot(unpacked(held[k, rows : rows + 16, :], rows), tile, 1, 0)
        to_near[k] = dot(far_dirs, tile, 1, 1)
    to_far[0] = total[:, 0:rows].astype(to_far.dtype)
    to_far[1] = total[:, rows:].astype(to_far.dtype)


def tiles(group, first, second, rhs):
    rows = first.shape[0] - 16
    vmem = pl.BlockSpec(memory_space=pltpu.VMEM)
    hbm = pl.BlockSpec(memory_space=pl.ANY)
    return pl.pallas_call(
        tiles_kernel,
        out_shape=(
            jax.ShapeDtypeStruct((ROUNDS, rhs, rows), jnp.bfloat16),
            jax.ShapeDtypeStruct((GROUP, rhs, rows), jnp.float32),
        ),
        in_specs=[hbm] * (ROUNDS + GROUP),
        out_specs=(vmem, vmem),
        scratch_shapes=[
            pltpu.VMEM((2 * rows, DESC), jnp.bfloat16),
            pltpu.VMEM((ROUNDS, 16, DESC), jnp.bfloat16),
            pltpu.VMEM((GROUP, *first.shape), jnp.bfloat16),
            pltpu.SemaphoreType.DMA((4 + GROUP,)),
        ],
        compiler_params=pltpu.CompilerParams(vmem_limit_bytes=24 * 1024 * 1024),
        cost_estimate=pl.CostEstimate(
            flops=16 * rows * rows * (DESC + 2 * rhs),
            bytes_accessed=6 * rows * DESC * 2,
            transcendentals=0,
        ),
    )(first, second, *group)


def pick(index, count, branch_of, *operands):
    return lax.switch(index, [branch_of(i) for i in range(count)], *operands)


def side_step(side, value):
    return pick(side, SIDE, lambda s: lambda v: beside(v, s), value)


def exchanged(value, axis, groups):
    return lax.all_to_all(value, axis, 0, 0, axis_index_groups=groups)


def on_device(descriptors, directions, ridge, partner):
    rhs, rows = directions.shape
    weight = (ROUNDS * rows * ROW) ** (-0.5)
    packed, (far0, side0, far1, side1) = start(partner, descriptors, directions)

    def near_and_side(nears):
        def branch(side, value, *values):
            near = [moved(v, near_pairs(k)) for v, k in zip(values, nears)]
            return *near, side_step(side, value)

        return branch

    def unmoved(side, value, *values):
        return *values, value

    def out_first(far):
        def branch(value, side):
            behind = lax.cond(
                side < SIDE, near_and_side((1, 3)), unmoved, side, value, value, value
            )
            return *behind, moved(value, far_pairs(far))

        return branch

    def out_second(far):
        def branch(first, second, packed, side):
            behind = lax.cond(side < SIDE, near_and_side((2,)), unmoved, side, first, packed)
            return *behind, moved(second, second_pairs(far))

        return branch

    def back_both(step):
        def branch(first, second, other):
            second = pick(other, STEPS, lambda f: lambda v: moved(v, second_back_pairs(f)), second)
            return second, moved(first, back_pairs(step if step < 7 else step + 3))

        return branch

    near1, near3, second, first = pick(far0, STEPS, out_first, packed, side1)
    near2, first, second = pick(far1, STEPS, out_second, first, second, packed, side0)
    to_far, to_near = tiles([packed, near1, near2, near3], first, second, rhs)
    half = moved(to_near[2:], near_pairs(2))
    second, first = pick(far0, STEPS, back_both, to_far[0], to_far[1], far1)
    env = lax.axis_index("env")
    place = (env >> 4) << 1 | (env & 1)
    slots = jnp.arange(SIDE, dtype=jnp.int32)[:, None, None]
    first, second, half = lax.optimization_barrier((first, second, half))
    to_near = to_near[:2] + half
    none = jnp.zeros_like(first)
    sent = jnp.where(slots == place ^ side0, first, none)
    sent = sent + jnp.where(slots == place ^ side1, second, none)
    side = exchanged(sent, "env", side_groups())
    result = to_near[0] + moved(to_near[1], near_pairs(1)) + jnp.sum(side.astype(jnp.float32), axis=0)
    return ridge[:, None] * directions.astype(jnp.float32) + weight * result


def solution(mesh):
    return jax.shard_map(
        on_device,
        mesh=mesh,
        in_specs=(P(("env", "row"), None), P(None, ("env", "row")), P(), P()),
        out_specs=P(None, ("env", "row")),
        check_vma=False,
    )
```
